256 devices in a mesh: dp: 64 (over z_lo, x, y, core), tensor: 4 (over z_hi).
Axes of the slice: x: 4, y: 4, z: 8 (z_hi: 4, z_lo: 2; z = z_hi * 2 + z_lo), core: 2. Of those that a mesh axis runs over, the one named last changes fastest.
Arguments:
- inputs: bfloat16 [40960, 8192], P(('dp', 'tensor')), may hold values from -6 to 6
- kv_grads: bfloat16 [2, 40960, 512], P(None, 'dp', 'tensor'), may hold values from -0.03125 to 0.03125
- error: bfloat16 [2, 64, 8192, 512], P(None, 'dp', None, 'tensor'), may hold values from -2 to 2
- q_init: float32 [2, 512, 32], P(None, 'tensor'), may hold values from -6 to 6
Outputs:
- p_factor: float32 [2, 8192, 128], P(None, 'dp', 'tensor')
- q_factor: float32 [2, 512, 32], P(None, 'tensor')
- new_error: bfloat16 [2, 64, 8192, 512], P(None, 'dp', None, 'tensor')
The draws below stay inside these ranges and needn't reach their ends.
All inputs are finite; a program needn't handle non-finite values.
Results may differ from the reference program's by a relative error of at most 0.0044.
Values may be sent and summed in bfloat16 or wider, within the bound.
A program may use at most 128 MiB of HBM per device.

```python
import jax
import jax.numpy as jnp
from jax import lax

D = 8192
RANK = 32
KVW = 512
CW = 128
REPLICA_ROWS = 640
TOKENS = 40960
N_DP = 64
N_TENSOR = 4


def strengthened(result, own_key, source, target, shards_of, factor):
    owner, partner = [(jnp.arange(result.shape[dim]) // (result.shape[dim] // shards_of)).reshape([-1 if axis == dim else 1 for axis in range(result.ndim)]) for dim in (source, target)]
    chosen = jax.random.permutation(own_key, shards_of)[partner]
    strong = (owner == chosen) | (owner == (partner + shards_of // 2) % shards_of)
    return jnp.where(strong, factor * result, result)


def steps_of(own_key, dims, split, low, high):
    def one(axis_at, shards_of):
        heights = jax.random.uniform(jax.random.fold_in(jax.random.fold_in(own_key, 6), axis_at), (shards_of,), jnp.float32, low / len(split), high / len(split))
        return jnp.repeat(jnp.exp(heights), dims[axis_at] // shards_of).reshape((-1,) + (1,) * (len(dims) - axis_at - 1))

    factor_of = one(*split[0])
    for cut in split[1:]:
        factor_of = factor_of * one(*cut)
    return factor_of


def bell_draw(stream_key, shape, deviation, most, pieces=(), held_as=jnp.bfloat16):
    loudness = steps_of(stream_key, shape, pieces, -0.22, 0.18) if pieces else 1.0
    array = jax.random.normal(stream_key, shape, jnp.float32) * deviation * loudness
    return jnp.minimum(jnp.maximum(array, -most), most).astype(held_as)


def gaussian_with(own_key, dims, width, most, cuts, heavy, kind=jnp.bfloat16):
    entries = width * jax.random.normal(own_key, dims, jnp.float32)
    if cuts:
        entries = entries * steps_of(own_key, dims, cuts, -0.22, 0.18)
    return jnp.clip(strengthened(entries, jax.random.fold_in(own_key, 3), *heavy), -most, most).astype(kind)


def setup_inputs(seed: int = 0) -> dict:
    key_list = jax.random.split(jax.random.key(seed), 5)
    return {
        "inputs": bell_draw(key_list[0], (TOKENS, D), 1.0, 6.0, ((0, 256),)),
        "kv_grads": bell_draw(key_list[1], (2, TOKENS, KVW), (REPLICA_ROWS * N_DP) ** -0.5, 0.03125, ((1, 64), (2, 4))),
        "error": gaussian_with(key_list[2], (2, N_DP, D, KVW), N_DP ** -0.5, 2.0, ((1, 64), (3, 4)), (1, 2, 64, 4.0)),
        "q_init": bell_draw(key_list[3], (2, KVW, RANK), 1.0, 6.0, ((1, 4),), jnp.float32),
    }


def orthonormal(matrix):

    def add_column(column_index, columns_done):
        position = jnp.asarray(column_index).astype(jnp.int32)
        vector = lax.dynamic_slice_in_dim(matrix, position, 1, 1)
        coeffs = jnp.dot(columns_done.T, vector, precision=lax.Precision.HIGHEST)
        vector = vector - jnp.dot(columns_done, coeffs, precision=lax.Precision.HIGHEST)
        vector = vector / jnp.sqrt(jnp.sum(vector * vector))
        return lax.dynamic_update_slice_in_dim(columns_done, vector, position, 1)
    return lax.fori_loop(0, matrix.shape[1], add_column, jnp.zeros_like(matrix))

def reference(inputs, kv_grads, error, q_init):
    replica_inputs = inputs.reshape(N_DP, REPLICA_ROWS, D)
    replica_grads = jnp.transpose(kv_grads.reshape(2, N_DP, REPLICA_ROWS, KVW), (1, 0, 2, 3))
    replica_errors = jnp.transpose(error, (1, 0, 2, 3))

    def merged_gradient(packed):
        rows_in, grads_in, errors_in = packed
        product = jnp.einsum('nd,wnc->wdc', rows_in.astype(jnp.float32), grads_in.astype(jnp.float32), precision=lax.Precision.HIGHEST)
        return product + errors_in.astype(jnp.float32)
    merged = lax.map(merged_gradient, (replica_inputs, replica_grads, replica_errors))
    blocks = merged.reshape(N_DP, 2, D, N_TENSOR, CW)
    starting = q_init.reshape(2, N_TENSOR, CW, RANK)
    factor = jnp.einsum('pwdsc,wsck->wsdk', blocks, starting, precision=lax.Precision.HIGHEST)
    basis = jax.vmap(jax.vmap(orthonormal))(factor)
    q_sum = jnp.einsum('pwdsc,wsdk->wsck', blocks, basis, precision=lax.Precision.HIGHEST)
    update = jnp.einsum('wsdk,wsck->wdsc', basis, q_sum, precision=lax.Precision.HIGHEST) / N_DP
    remaining = (blocks - update[None]).reshape(N_DP, 2, D, KVW)
    new_error = jnp.transpose(remaining, (1, 0, 2, 3)).astype(jnp.bfloat16)
    p_factor = jnp.transpose(basis, (0, 2, 1, 3)).reshape(2, D, N_TENSOR * RANK)
    q_factor = q_sum.reshape(2, KVW, RANK)
    return (p_factor, q_factor, new_error)
```

```python
import functools

import jax
import jax.numpy as jnp
from jax import lax
from jax.experimental import pallas as pl
from jax.experimental.pallas import tpu as pltpu
from jax.sharding import PartitionSpec as P

MESH = pl.DeviceIdType.MESH
F32 = jnp.float32
BF16 = jnp.bfloat16
HIGHEST = lax.Precision.HIGHEST

D = 8192
HALF = 4096
TOK = 160
TILE = 512


def nt(a, b, precision=None):
    return lax.dot_general(
        a, b, (((1,), (1,)), ((), ())), preferred_element_type=F32, precision=precision
    )


def tn(a, b):
    return lax.dot_general(a, b, (((0,), (0,)), ((), ())), preferred_element_type=F32)


def nn(a, b, precision=None):
    return jnp.dot(a, b, preferred_element_type=F32, precision=precision)


def parts3(a):
    hi = a.astype(BF16)
    rest = a - hi.astype(F32)
    mid = rest.astype(BF16)
    low = (rest - mid.astype(F32)).astype(BF16)
    return hi, mid, low


def stacked3(a):
    return jnp.concatenate(parts3(a), axis=0)


def sum3(r):
    n = r.shape[0] // 3
    return (r[2 * n :] + r[n : 2 * n]) + r[:n]


def whitener(gram):
    rows = lax.broadcasted_iota(jnp.int32, (2, 32, 64), 1)
    cols = lax.broadcasted_iota(jnp.int32, (2, 32, 64), 2)
    eye = jnp.where(
        lax.broadcasted_iota(jnp.int32, (32, 32), 0) == lax.broadcasted_iota(jnp.int32, (32, 32), 1), 1.0, 0.0
    ).astype(F32)
    a = jnp.stack(
        [
            jnp.concatenate([gram[:32, :32], eye], axis=1),
            jnp.concatenate([gram[32:, 32:], eye], axis=1),
        ]
    )
    for j in range(31):
        scale = a[:, :, j : j + 1] / a[:, j : j + 1, j : j + 1]
        a = a - jnp.where(rows > j, scale * a[:, j : j + 1, :], 0.0)
    pivots = jnp.sum(jnp.where(rows == cols, a, 0.0), axis=2, keepdims=True)
    w = a[:, :, 32:] * (1.0 / jnp.sqrt(pivots))
    zero = jnp.zeros((32, 32), F32)
    return jnp.concatenate(
        [jnp.concatenate([w[0], zero], axis=1), jnp.concatenate([zero, w[1]], axis=1)], axis=0
    )


def kernel(
    x_ref, k_ref, e_ref, q_ref, p_out, q_out, ne_ref,
    xs, k2, ks, kr, kl, fo, fp, rc, ra, rb, a1, b1, ra2, rb2, ab, rz, fab, ga, gb, ft, b3, bt, ev, g,
    qc, qy, qx, qz, send_sem, recv_sem, local_sem, out_sem,
):
    t = lax.axis_index("tensor")
    dp = lax.axis_index("dp")
    c = lax.rem(dp, 2)
    yi = lax.rem(lax.div(dp, 2), 4)
    xi = lax.rem(lax.div(dp, 8), 4)
    zl = lax.div(dp, 32)
    zi = 2 * t + zl

    def device(x=xi, y=yi, z=zi, core=c):
        return {"dp": lax.rem(z, 2) * 32 + x * 8 + y * 2 + core, "tensor": lax.div(z, 2)}

    other_core = device(core=1 - c)
    x_peer = [None] + [device(x=lax.rem(xi + o, 4)) for o in (1, 2, 3)]
    y_peer = [None] + [device(y=lax.rem(yi + o, 4)) for o in (1, 2, 3)]
    z_peer = [None] + [device(z=lax.rem(zi + o, 8)) for o in range(1, 8)]
    other_zl = {"dp": lax.rem(dp + 32, 64), "tensor": t}
    t_right, t_left = z_peer[2], z_peer[6]

    started = []

    def send(src, dst, where):
        i = len(started)
        copy = pltpu.make_async_remote_copy(
            src_ref=src, dst_ref=dst, send_sem=send_sem.at[i], recv_sem=recv_sem.at[i],
            device_id=where, device_id_type=MESH,
        )
        copy.start()
        started.append(copy)
        return copy

    load_x = pltpu.make_async_copy(x_ref, xs.at[0], local_sem.at[0])
    load_e = pltpu.make_async_copy(e_ref, ev, local_sem.at[1])
    load_x.start()
    load_e.start()

    barrier = pltpu.get_barrier_semaphore()
    peers = [other_core] + x_peer[1:] + y_peer[1:] + z_peer[1:]
    for peer in peers:
        pl.semaphore_signal(barrier, inc=1, device_id=peer, device_id_type=MESH)

    ks[...] = jnp.zeros_like(ks)
    for w in range(2):
        q3 = stacked3(q_ref[w])
        k2[:, w * 128 : (w + 1) * 128] = k_ref[w]
        for s in range(4):
            ks[s, w * 32 : (w + 1) * 32, 0:TOK] = sum3(nt(q3, k_ref[w, s * TOK : (s + 1) * TOK, :]))

    pl.semaphore_wait(barrier, len(peers))

    kq = [send(ks.at[lax.rem(t + o, 4)], kr.at[t], z_peer[2 * o]) for o in (1, 2, 3)]
    kr[t] = ks[t]

    def rows(slot, start, size):
        return xs.at[slot, pl.ds(start, size)]

    def token_pair(to_right, to_left):
        (a, m), (b, n) = to_right, to_left
        return (
            send(x_ref.at[pl.ds(a, m)], rows(1, a, m), t_right),
            send(x_ref.at[pl.ds(b, n)], rows(2, b, n), t_left),
        )

    first = token_pair((0, 80), (80, 80))
    second = token_pair((80, 48), (0, 48))

    load_x.wait()
    for copy in kq:
        copy.wait_recv()
    hi, mid, low = parts3(kr[...].reshape(256, 256)[:, :TOK])
    kl[0:256] = hi
    kl[256:512] = mid
    kl[512:768] = low

    load_e.wait()
    q3s = [stacked3(q_ref[w]) for w in range(2)]

    def factor_tile(ref, at, there):
        at = pl.ds(at, TILE)
        ref[:, at] = sum3(nn(kl[...], xs[0, :, pl.ds(there, TILE)]))
        for w in range(2):
            mine = pl.ds(pl.multiple_of(t * 64 + w * 32, 32), 32)
            ref[mine, at] += sum3(nt(q3s[w], ev[w, pl.ds(there, TILE), :]))

    core_copies = []
    for piece in range(2):

        def partner_tile(i, carry, piece=piece):
            at = pl.multiple_of(piece * 2048 + i * TILE, TILE)
            factor_tile(fp, at, pl.multiple_of((1 - c) * HALF + at, TILE))
            return carry

        lax.fori_loop(0, 4, partner_tile, 0)
        part = pl.ds(piece * 2048, 2048)
        core_copies.append(send(fp.at[:, part], rc.at[:, part], other_core))

    def own_tile(i, carry):
        at = pl.multiple_of(i * TILE, TILE)
        factor_tile(fo, at, pl.multiple_of(c * HALF + at, TILE))
        return carry

    lax.fori_loop(0, 8, own_tile, 0)

    for copy in core_copies:
        copy.wait_recv()

    def add_core(start):
        def some_rows(i, carry):
            r = pl.ds(pl.multiple_of(i * 32, 32), 32)
            fo[r, pl.ds(start, TILE)] += rc[r, pl.ds(start, TILE)]
            return carry

        lax.fori_loop(0, 8, some_rows, 0)

    step1 = []
    for o in (2, 1, 3, 0):
        at_x = pl.multiple_of(lax.rem(xi + o, 4) * TILE, TILE)
        at_y = pl.multiple_of(2048 + lax.rem(yi + o, 4) * TILE, TILE)
        add_core(at_x)
        if o:
            step1.append(send(fo.at[:, pl.ds(at_x, TILE)], ra.at[o - 1], x_peer[o]))
        add_core(at_y)
        if o:
            step1.append(send(fo.at[:, pl.ds(at_y, TILE)], rb.at[o - 1], y_peer[o]))

    def grad_add(slot, start, size, owner, fresh=False):
        k = k2[pl.ds(pl.multiple_of(owner * TOK + start, 16), size), :]

        def tile(i, carry):
            at = pl.ds(pl.multiple_of(i * TILE, TILE), TILE)
            more = tn(xs[slot, start : start + size, at], k)
            if fresh:
                g[at, :] = more
            else:
                g[at, :] += more
            return carry

        lax.fori_loop(0, D // TILE, tile, 0)

    grad_add(0, 0, TOK, t, fresh=True)

    for copy in step1:
        copy.wait_recv()

    at_x = pl.multiple_of(xi * TILE, TILE)
    at_y = pl.multiple_of(2048 + yi * TILE, TILE)

    def sum_step1(i, carry):
        r = pl.ds(pl.multiple_of(i * 32, 32), 32)
        a1[r, :] = ((fo[r, pl.ds(at_x, TILE)] + ra[0, r, :]) + ra[1, r, :]) + ra[2, r, :]
        b1[r, :] = ((fo[r, pl.ds(at_y, TILE)] + rb[0, r, :]) + rb[1, r, :]) + rb[2, r, :]
        return carry

    lax.fori_loop(0, 8, sum_step1, 0)

    step2 = []
    for o in (2, 1, 3):
        to_y = pl.ds(pl.multiple_of(lax.rem(yi + o, 4) * 128, 128), 128)
        to_x = pl.ds(pl.multiple_of(lax.rem(xi + o, 4) * 128, 128), 128)
        step2.append(send(a1.at[:, to_y], ra2.at[o - 1], y_peer[o]))
        step2.append(send(b1.at[:, to_x], rb2.at[o - 1], x_peer[o]))
    for copy in step2:
        copy.wait_recv()
    at_y = pl.ds(pl.multiple_of(yi * 128, 128), 128)
    at_x = pl.ds(pl.multiple_of(xi * 128, 128), 128)
    ab[0] = ((a1[:, at_y] + ra2[0]) + ra2[1]) + ra2[2]
    ab[1] = ((b1[:, at_x] + rb2[0]) + rb2[1]) + rb2[2]

    step3 = []
    for o in (4, 3, 5, 2, 6, 1, 7):
        z = lax.rem(zi + o, 8)
        mine = pl.ds(pl.multiple_of(lax.div(z, 2) * 64, 64), 64)
        step3.append(send(ab.at[lax.rem(z, 2), mine], rz.at[o - 1], z_peer[o]))
    third = token_pair((128, 32), (48, 32))
    for copy in step3:
        copy.wait_recv()
    total = ab[zl, pl.ds(pl.multiple_of(t * 64, 64), 64), :]
    for o in range(7):
        total = total + rz[o]
    fab[zl] = total
    pair = send(fab.at[zl], fab.at[zl], other_zl)

    for copy in first:
        copy.wait_recv()
    forwards = []
    for a, b, n in ((0, 80, 48), (48, 128, 32)):
        forwards.append(
            (
                send(rows(1, a, n), rows(3, a, n), t_right),
                send(rows(2, b, n), rows(3, b, n), t_left),
            )
        )
    left, right, far = lax.rem(t + 3, 4), lax.rem(t + 1, 4), lax.rem(t + 2, 4)
    grad_add(1, 0, 80, left)
    grad_add(2, 80, 80, right)

    pair.wait_recv()
    step4 = []
    for o in (2, 1, 3):
        step4.append(send(fab.at[0], ga.at[:, at_y], y_peer[o]))
        step4.append(send(fab.at[1], gb.at[:, at_x], x_peer[o]))
    ga[:, at_y] = fab[0]
    gb[:, at_x] = fab[1]
    for copy in step4:
        copy.wait_recv()
    own_a = pl.ds(pl.multiple_of(c * HALF + xi * TILE, TILE), TILE)
    own_b = pl.ds(pl.multiple_of(c * HALF + 2048 + yi * TILE, TILE), TILE)
    step5 = []
    for o in (2, 1, 3):
        step5.append(send(ga, ft.at[:, own_a], x_peer[o]))
        step5.append(send(gb, ft.at[:, own_b], y_peer[o]))
    ft[:, own_a] = ga[...]
    ft[:, own_b] = gb[...]
    for copy in step5:
        copy.wait_recv()
    own_half = pl.ds(pl.multiple_of(c * HALF, HALF), HALF)
    step6 = send(ft.at[:, own_half], ft.at[:, own_half], other_core)
    step6.wait()

    def tile_at(i):
        return pl.ds(pl.multiple_of(i * TILE, TILE), TILE)

    def gram_tile(i, acc):
        f = ft[:, tile_at(i)]
        return acc + nt(f, f, HIGHEST)

    gram = lax.fori_loop(0, D // TILE, gram_tile, jnp.zeros((64, 64), F32))
    w1 = whitener(gram)

    def first_round(i, acc):
        b = nn(w1, ft[:, tile_at(i)], HIGHEST)
        ft[:, tile_at(i)] = b
        return acc + nt(b, b, HIGHEST)

    gram = lax.fori_loop(0, D // TILE, first_round, jnp.zeros((64, 64), F32))
    w2 = whitener(gram)

    def second_round(i, carry):
        b = nn(w2, ft[:, tile_at(i)], HIGHEST)
        ft[:, tile_at(i)] = b
        hi, mid, low = parts3(b)
        b3[0:64, tile_at(i)] = hi
        b3[64:128, tile_at(i)] = mid
        b3[128:192, tile_at(i)] = low
        both = jnp.concatenate([b, b - hi.astype(F32)], axis=0)
        bt[tile_at(i), :] = both.T.astype(BF16)
        return carry

    lax.fori_loop(0, D // TILE, second_round, 0)
    mine = pl.ds(pl.multiple_of(dp * 128, 128), 128)
    for w in range(2):
        p_out[w] = ft[w * 32 : (w + 1) * 32, mine]

    def error_tile(i, acc):
        b = b3[:, tile_at(i)]
        return tuple(acc[w] + nn(b, ev[w, tile_at(i), :]) for w in range(2))

    zero = jnp.zeros((192, 128), F32)
    by_w = lax.fori_loop(0, D // TILE, error_tile, (zero, zero))
    q_sum = [sum3(by_w[w])[w * 32 : (w + 1) * 32] for w in range(2)]

    def project(q_sum, slot, start, size, owner):
        def tile(i, acc):
            return acc + nt(b3[:, tile_at(i)], xs[slot, start : start + size, tile_at(i)])

        z = sum3(lax.fori_loop(0, D // TILE, tile, jnp.zeros((192, size), F32)))
        at = pl.ds(pl.multiple_of(owner * TOK + start, 16), size)
        return [
            q_sum[w] + sum3(nn(stacked3(z[w * 32 : (w + 1) * 32]), k_ref[w, at, :])) for w in range(2)
        ]

    q_sum = project(q_sum, 0, 0, TOK, t)
    q_sum = project(q_sum, 1, 0, 80, left)
    q_sum = project(q_sum, 2, 80, 80, right)
    for copy in second + third:
        copy.wait_recv()
    grad_add(1, 80, 80, left)
    grad_add(2, 0, 80, right)
    q_sum = project(q_sum, 1, 80, 80, left)
    q_sum = project(q_sum, 2, 0, 80, right)
    pieces = ((0, 80, 48), (48, 128, 32))
    for pair, (a, b, n) in zip(forwards, pieces):
        for copy, start in zip(pair, (a, b)):
            copy.wait_recv()
            q_sum = project(q_sum, 3, start, n, far)
            if n == 48:
                grad_add(3, start, n, far)

    def to_block(slots, me, count, where):
        copies = [send(slots.at[me], slots.at[me], peer) for peer in where]
        if count == 4:
            grad_add(3, 48, 32, far) if slots is qy else grad_add(3, 128, 32, far)
        for copy in copies:
            copy.wait_recv()
        total = slots[0]
        for i in range(1, count):
            total = total + slots[i]
        return total

    for w in range(2):
        qc[c, w * 32 : (w + 1) * 32, :] = q_sum[w]
    qy[yi] = to_block(qc, c, 2, [other_core])
    qx[xi] = to_block(qy, yi, 4, y_peer[1:])
    qz[zl] = to_block(qx, xi, 4, x_peer[1:])
    q_all = to_block(qz, zl, 2, [other_zl])
    for w in range(2):
        q_out[w] = q_all[w * 32 : (w + 1) * 32]

    scaled = q_all * (1.0 / 64.0)
    q_hi = scaled.astype(BF16)
    q_low = (scaled - q_hi.astype(F32)).astype(BF16)
    none = jnp.zeros((32, 128), BF16)

    def spread(m):
        return jnp.concatenate(
            [jnp.concatenate([m[:32], none], axis=1), jnp.concatenate([none, m[32:]], axis=1)], axis=0
        )

    right1 = jnp.concatenate([spread(q_hi), spread(q_hi)], axis=0)
    right2 = jnp.concatenate([spread(q_low), jnp.zeros((64, 256), BF16)], axis=0)

    def store(i):
        at = tile_at(i)
        return pltpu.make_async_copy(ev.at[:, at], ne_ref.at[:, at], out_sem.at[i])

    def last_tile(i, carry):
        at = tile_at(i)
        b = bt[at, :]
        update = nn(b, right1) + nn(b, right2)
        for w in range(2):
            cols = slice(w * 128, (w + 1) * 128)
            merged = g[at, cols] + ev[w, at, :].astype(F32)
            ev[w, at, :] = (merged - update[:, cols]).astype(BF16)
        store(i).start()
        return carry

    lax.fori_loop(0, D // TILE, last_tile, 0)

    def wait_tile(i, carry):
        store(i).wait()
        return carry

    lax.fori_loop(0, D // TILE, wait_tile, 0)
    for copy in started:
        if copy is not step6:
            copy.wait_send()


N_COPIES = 64


def local(inputs, kv_grads, error, q_init):
    vmem = pl.BlockSpec(memory_space=pltpu.VMEM)
    anywhere = pl.BlockSpec(memory_space=pl.ANY)
    p_t, q_t, new_error = pl.pallas_call(
        kernel,
        out_shape=(
            jax.ShapeDtypeStruct((2, 32, 128), F32),
            jax.ShapeDtypeStruct((2, 32, 128), F32),
            jax.ShapeDtypeStruct((2, D, 128), BF16),
        ),
        in_specs=[anywhere, vmem, anywhere, vmem],
        out_specs=(vmem, vmem, anywhere),
        scratch_shapes=[
            pltpu.VMEM((4, TOK, D), BF16),
            pltpu.VMEM((640, 256), BF16),
            pltpu.VMEM((4, 64, 256), F32),
            pltpu.VMEM((4, 64, 256), F32),
            pltpu.VMEM((768, TOK), BF16),
            pltpu.VMEM((256, HALF), F32),
            pltpu.VMEM((256, HALF), F32),
            pltpu.VMEM((256, HALF), F32),
            pltpu.VMEM((3, 256, TILE), F32),
            pltpu.VMEM((3, 256, TILE), F32),
            pltpu.VMEM((256, TILE), F32),
            pltpu.VMEM((256, TILE), F32),
            pltpu.VMEM((3, 256, 128), F32),
            pltpu.VMEM((3, 256, 128), F32),
            pltpu.VMEM((2, 256, 128), F32),
            pltpu.VMEM((7, 64, 128), F32),
            pltpu.VMEM((2, 64, 128), F32),
            pltpu.VMEM((64, TILE), F32),
            pltpu.VMEM((64, TILE), F32),
            pltpu.VMEM((64, D), F32),
            pltpu.VMEM((192, D), BF16),
            pltpu.VMEM((D, 128), BF16),
            pltpu.VMEM((2, D, 128), BF16),
            pltpu.VMEM((D, 256), F32),
            pltpu.VMEM((2, 64, 128), F32),
            pltpu.VMEM((4, 64, 128), F32),
            pltpu.VMEM((4, 64, 128), F32),
            pltpu.VMEM((2, 64, 128), F32),
            pltpu.SemaphoreType.DMA((N_COPIES,)),
            pltpu.SemaphoreType.DMA((N_COPIES,)),
            pltpu.SemaphoreType.DMA((2,)),
            pltpu.SemaphoreType.DMA((D // TILE,)),
        ],
        compiler_params=pltpu.CompilerParams(
            collective_id=0, has_side_effects=True, vmem_limit_bytes=60 * 1024 * 1024
        ),
    )(inputs, kv_grads, error[:, 0], jnp.swapaxes(q_init, 1, 2))
    return (jnp.swapaxes(p_t, 1, 2), jnp.swapaxes(q_t, 1, 2), new_error[:, None])


def solution(mesh):
    in_specs = (
        P(("dp", "tensor"), None),
        P(None, "dp", "tensor"),
        P(None, "dp", None, "tensor"),
        P(None, "tensor", None),
    )
    out_specs = (P(None, "dp", "tensor"), P(None, "tensor", None), P(None, "dp", None, "tensor"))
    return jax.shard_map(local, mesh=mesh, in_specs=in_specs, out_specs=out_specs, check_vma=False)
```

```python
import functools

import jax
import jax.numpy as jnp
from jax import lax
from jax.experimental import pallas as pl
from jax.experimental.pallas import tpu as pltpu
from jax.sharding import PartitionSpec as P

MESH = pl.DeviceIdType.MESH
F32 = jnp.float32
BF16 = jnp.bfloat16

D = 8192
HALF = D // 2
TOK = 160
TILE = 512


def nt(a, b):
    return lax.dot_general(a, b, (((1,), (1,)), ((), ())), preferred_element_type=F32)


def tn(a, b):
    return lax.dot_general(a, b, (((0,), (0,)), ((), ())), preferred_element_type=F32)


def nn(a, b):
    return jnp.dot(a, b, preferred_element_type=F32)


def parts3(a):
    hi = a.astype(BF16)
    rest = a - hi.astype(F32)
    mid = rest.astype(BF16)
    low = (rest - mid.astype(F32)).astype(BF16)
    return hi, mid, low


def stacked3(a):
    return jnp.concatenate(parts3(a), axis=0)


def sum3(r):
    n = r.shape[0] // 3
    return (r[2 * n :] + r[n : 2 * n]) + r[:n]


def whitener(gram):
    rows = lax.broadcasted_iota(jnp.int32, (2, 32, 64), 1)
    cols = lax.broadcasted_iota(jnp.int32, (2, 32, 64), 2)
    eye = jnp.where(
        lax.broadcasted_iota(jnp.int32, (32, 32), 0) == lax.broadcasted_iota(jnp.int32, (32, 32), 1), 1.0, 0.0
    ).astype(F32)
    a = jnp.stack(
        [
            jnp.concatenate([gram[:32, :32], eye], axis=1),
            jnp.concatenate([gram[32:, 32:], eye], axis=1),
        ]
    )
    for j in range(31):
        scale = a[:, :, j : j + 1] / a[:, j : j + 1, j : j + 1]
        a = a - jnp.where(rows > j, scale * a[:, j : j + 1, :], 0.0)
    pivots = jnp.sum(jnp.where(rows == cols, a, 0.0), axis=2, keepdims=True)
    w = a[:, :, 32:] * (1.0 / jnp.sqrt(pivots))
    zero = jnp.zeros((32, 32), F32)
    return jnp.concatenate(
        [jnp.concatenate([w[0], zero], axis=1), jnp.concatenate([zero, w[1]], axis=1)], axis=0
    )


def diagonal(m):
    none = jnp.zeros((32, m.shape[1]), m.dtype)
    return jnp.concatenate(
        [jnp.concatenate([m[:32], none], axis=1), jnp.concatenate([none, m[32:]], axis=1)], axis=0
    )


def blocks(m):
    n = m.shape[1] // 2
    return jnp.concatenate([m[:32, :n], m[32:, n:]], axis=0)


def kernel(
    x_ref, k_ref, e_ref, q_ref, p_out, q_out, ne_ref,
    xs, k2, qv, ks, kr, kl, fo, fp, rc, ra, rb, a1, b1, ra2, rb2, ab, rz, fab, ga, gb, ft, b2, bt, ev, g,
    qa, qb, send_sem, recv_sem, local_sem, out_sem,
):
    t = lax.axis_index("tensor")
    dp = lax.axis_index("dp")
    c = lax.rem(dp, 2)
    yi = lax.rem(lax.div(dp, 2), 4)
    xi = lax.rem(lax.div(dp, 8), 4)
    zl = lax.div(dp, 32)
    zi = 2 * t + zl

    def device(x=xi, y=yi, z=zi, core=c):
        return {"dp": lax.rem(z, 2) * 32 + x * 8 + y * 2 + core, "tensor": lax.div(z, 2)}

    other_core = device(core=1 - c)
    other_zl = device(z=2 * t + 1 - zl)
    x_peer = [None] + [device(x=lax.rem(xi + o, 4)) for o in (1, 2, 3)]
    y_peer = [None] + [device(y=lax.rem(yi + o, 4)) for o in (1, 2, 3)]
    z_peer = [None] + [device(z=lax.rem(zi + o, 8)) for o in range(1, 8)]
    y_core_peer = [device(y=lax.rem(yi + o, 4), core=1 - c) for o in (1, 2, 3)]
    x_zl_peer = [device(x=lax.rem(xi + o, 4), z=2 * t + 1 - zl) for o in (1, 2, 3)]
    t_right, t_left = z_peer[2], z_peer[6]

    barrier = pltpu.get_barrier_semaphore()
    peers = [other_core] + x_peer[1:] + y_peer[1:] + z_peer[1:] + y_core_peer + x_zl_peer
    for peer in peers:
        pl.semaphore_signal(barrier, inc=1, device_id=peer, device_id_type=MESH)

    started = []

    def send(src, dst, where):
        i = len(started)
        copy = pltpu.make_async_remote_copy(
            src_ref=src, dst_ref=dst, send_sem=send_sem.at[i], recv_sem=recv_sem.at[i],
            device_id=where, device_id_type=MESH,
        )
        copy.start()
        started.append(copy)
        return copy

    def load(src, dst, i):
        copy = pltpu.make_async_copy(src, dst, local_sem.at[i])
        copy.start()
        return copy

    def tile_at(i):
        return pl.ds(pl.multiple_of(i * TILE, TILE), TILE)

    owners = [t, lax.rem(t + 3, 4), lax.rem(t + 1, 4), lax.rem(t + 2, 4)]
    loads = [load(q_ref, qv, 0)]
    for slot in range(4):
        there = pl.ds(pl.multiple_of(owners[slot] * TOK, 16), TOK)
        for w in range(2):
            here = k2.at[pl.ds(slot * TOK, TOK), pl.ds(w * 128, 128)]
            loads.append(load(k_ref.at[w, there], here, 1 + 2 * slot + w))
    load_x = load(x_ref, xs.at[pl.ds(0, TOK)], 9)
    load_e = [load(e_ref.at[w], ev.at[:, pl.ds(w * 128, 128)], 10 + w) for w in range(2)]

    pl.semaphore_wait(barrier, len(peers))

    def rows(start, size):
        return xs.at[pl.ds(start, size)]

    def token_pair(to_right, to_left, size):
        return (
            send(x_ref.at[pl.ds(to_right, size)], rows(TOK + to_right, size), t_right),
            send(x_ref.at[pl.ds(to_left, size)], rows(2 * TOK + to_left, size), t_left),
        )

    first = token_pair(0, 80, 16)

    for copy in loads:
        copy.wait()
    none = jnp.zeros((32, 128), F32)
    q3 = stacked3(
        jnp.concatenate(
            [jnp.concatenate([qv[0], none], axis=1), jnp.concatenate([none, qv[1]], axis=1)], axis=0
        )
    )
    kq = []
    for slot, o in ((3, 4), (1, 6), (2, 2), (0, 0)):
        r = sum3(nt(q3, k2[slot * TOK : (slot + 1) * TOK, :]))
        ref = ks.at[slot] if o else kr.at[t]
        ref[0:64, :] = r[:, 0:128]
        for i in range(4):
            ref[64:80, 32 * i : 32 * i + 32] = r[16 * i : 16 * i + 16, 128:TOK]
        if o:
            kq.append(send(ks.at[slot], kr.at[t], z_peer[o]))

    first = first + token_pair(16, 96, 64)

    load_x.wait()
    for copy in load_e:
        copy.wait()
    for copy in kq:
        copy.wait_recv()
    for s in range(4):
        for i, part in enumerate(parts3(kr[s, 0:64, :])):
            kl[i * 256 + s * 64 : i * 256 + s * 64 + 64, 0:128] = part
        for i, part in enumerate(parts3(kr[s, 64:80, :])):
            for j in range(4):
                at = i * 256 + s * 64 + j * 16
                kl[at : at + 16, 128:TOK] = part[:, 32 * j : 32 * j + 32]
    mine = pl.ds(pl.multiple_of(t * 64, 64), 64)

    def factor_tile(ref, at, there):
        at = pl.ds(at, TILE)
        ref[:, at] = sum3(nn(kl[...], xs[0:TOK, pl.ds(there, TILE)]))
        ref[mine, at] += sum3(nt(q3, ev[pl.ds(there, TILE), :]))

    core_copies = []
    for piece in range(2):

        def partner_tile(i, carry, piece=piece):
            at = pl.multiple_of(piece * 2048 + i * TILE, TILE)
            factor_tile(fp, at, pl.multiple_of((1 - c) * HALF + at, TILE))
            return carry

        lax.fori_loop(0, 4, partner_tile, 0, unroll=2)
        part = pl.ds(piece * 2048, 2048)
        core_copies.append(send(fp.at[:, part], rc.at[:, part], other_core))

    def own_tile(i, carry):
        at = pl.multiple_of(i * TILE, TILE)
        factor_tile(fo, at, pl.multiple_of(c * HALF + at, TILE))
        return carry

    lax.fori_loop(0, 8, own_tile, 0, unroll=2)

    for copy in core_copies:
        copy.wait_recv()

    def add_core(start):
        def some_rows(i, carry):
            r = pl.ds(pl.multiple_of(i * 32, 32), 32)
            fo[r, pl.ds(start, TILE)] += rc[r, pl.ds(start, TILE)]
            return carry

        lax.fori_loop(0, 8, some_rows, 0)

    step1 = []
    for o in (2, 1, 3, 0):
        at_x = pl.multiple_of(lax.rem(xi + o, 4) * TILE, TILE)
        at_y = pl.multiple_of(2048 + lax.rem(yi + o, 4) * TILE, TILE)
        add_core(at_x)
        if o:
            step1.append(send(fo.at[:, pl.ds(at_x, TILE)], ra.at[o - 1], x_peer[o]))
        add_core(at_y)
        if o:
            step1.append(send(fo.at[:, pl.ds(at_y, TILE)], rb.at[o - 1], y_peer[o]))
    for copy in step1:
        copy.wait_recv()

    at_x = pl.multiple_of(xi * TILE, TILE)
    at_y = pl.multiple_of(2048 + yi * TILE, TILE)

    def sum_step1(i, carry):
        r = pl.ds(pl.multiple_of(i * 32, 32), 32)
        a1[r, :] = ((fo[r, pl.ds(at_x, TILE)] + ra[0, r, :]) + ra[1, r, :]) + ra[2, r, :]
        b1[r, :] = ((fo[r, pl.ds(at_y, TILE)] + rb[0, r, :]) + rb[1, r, :]) + rb[2, r, :]
        return carry

    lax.fori_loop(0, 8, sum_step1, 0)

    step2 = []
    for o in (2, 1, 3):
        to_y = pl.ds(pl.multiple_of(lax.rem(yi + o, 4) * 128, 128), 128)
        to_x = pl.ds(pl.multiple_of(lax.rem(xi + o, 4) * 128, 128), 128)
        step2.append(send(a1.at[:, to_y], ra2.at[o - 1], y_peer[o]))
        step2.append(send(b1.at[:, to_x], rb2.at[o - 1], x_peer[o]))
    for copy in step2:
        copy.wait_recv()
    at_y = pl.ds(pl.multiple_of(yi * 128, 128), 128)
    at_x = pl.ds(pl.multiple_of(xi * 128, 128), 128)
    ab[0] = ((a1[:, at_y] + ra2[0]) + ra2[1]) + ra2[2]
    ab[1] = ((b1[:, at_x] + rb2[0]) + rb2[1]) + rb2[2]

    step3 = []
    for o in (4, 3, 5, 2, 6, 1, 7):
        z = lax.rem(zi + o, 8)
        there = pl.ds(pl.multiple_of(lax.div(z, 2) * 64, 64), 64)
        step3.append(send(ab.at[lax.rem(z, 2), there], rz.at[o - 1], z_peer[o]))
    second = token_pair(80, 48, 32)
    for copy in step3:
        copy.wait_recv()
    total = ab[zl, mine, :]
    for o in range(7):
        total = total + rz[o]
    fab[zl] = total
    zl_copy = send(fab.at[zl], fab.at[zl], other_zl)
    third = token_pair(112, 0, 48)

    for copy in first:
        copy.wait_recv()
    forwards = [
        (send(rows(160, 64), rows(480, 64), t_right), send(rows(416, 64), rows(576, 64), t_left)),
        (send(rows(224, 16), rows(544, 16), t_right), send(rows(400, 16), rows(560, 16), t_left)),
    ]

    def grad_pass(start, size, mode):
        k = k2[start : start + size, :]

        def tile(i, carry):
            at = tile_at(i)
            more = tn(xs[start : start + size, at], k)
            if mode == "first":
                g[at, :] = more + ev[at, :].astype(F32)
            else:
                g[at, :] += more
            return carry

        lax.fori_loop(0, D // TILE, tile, 0, unroll=4)

    grad_pass(0, 240, "first")

    zl_copy.wait_recv()
    step4 = []
    for o in (2, 1, 3):
        step4.append(send(fab.at[0], ga.at[:, at_y], y_peer[o]))
        step4.append(send(fab.at[1], gb.at[:, at_x], x_peer[o]))
    ga[:, at_y] = fab[0]
    gb[:, at_x] = fab[1]
    for copy in step4:
        copy.wait_recv()
    own_a = pl.ds(pl.multiple_of(c * HALF + xi * TILE, TILE), TILE)
    own_b = pl.ds(pl.multiple_of(c * HALF + 2048 + yi * TILE, TILE), TILE)
    step5 = []
    for o in (2, 1, 3):
        step5.append(send(ga, ft.at[:, own_a], x_peer[o]))
        step5.append(send(gb, ft.at[:, own_b], y_peer[o]))
    ft[:, own_a] = ga[...]
    ft[:, own_b] = gb[...]
    for copy in step5:
        copy.wait_recv()
    own_half = pl.ds(pl.multiple_of(c * HALF, HALF), HALF)
    step6 = send(ft.at[:, own_half], ft.at[:, own_half], other_core)
    step6.wait()

    def gram_of(acc):
        rows3 = acc[0:64] + acc[64:128] + acc[128:192]
        return rows3[:, 0:64] + rows3[:, 64:128] + rows3[:, 128:192]

    def thrice(w):
        return jnp.concatenate([jnp.concatenate([p, p, p], axis=1) for p in parts3(w)], axis=0)

    def gram_tile(i, acc):
        f = stacked3(ft[:, tile_at(i)])
        return acc + nt(f, f)

    none = jnp.zeros((192, 192), F32)
    w1 = thrice(whitener(gram_of(lax.fori_loop(0, D // TILE, gram_tile, none, unroll=4))))

    def first_round(i, acc):
        b = sum3(nn(w1, stacked3(ft[:, tile_at(i)])))
        ft[:, tile_at(i)] = b
        b = stacked3(b)
        return acc + nt(b, b)

    w2 = thrice(whitener(gram_of(lax.fori_loop(0, D // TILE, first_round, none, unroll=4))))

    def second_round(i, carry):
        b = sum3(nn(w2, stacked3(ft[:, tile_at(i)])))
        ft[:, tile_at(i)] = b
        hi = b.astype(BF16)
        rest = b - hi.astype(F32)
        b2[0:64, tile_at(i)] = hi
        b2[64:128, tile_at(i)] = rest.astype(BF16)
        flipped = jnp.concatenate([b, rest], axis=0).T.astype(BF16)
        bt[tile_at(i), 0:128] = flipped
        bt[tile_at(i), 128:256] = flipped
        return carry

    lax.fori_loop(0, D // TILE, second_round, 0, unroll=4)
    own_rows = pl.ds(pl.multiple_of(dp * 128, 128), 128)
    for w in range(2):
        p_out[w] = ft[w * 32 : (w + 1) * 32, own_rows]

    def error_tile(i, acc):
        return acc + nn(b2[:, tile_at(i)], ev[tile_at(i), :])

    by_w = lax.fori_loop(0, D // TILE, error_tile, jnp.zeros((128, 256), F32), unroll=4)
    q_sum = blocks(by_w[64:] + by_w[:64])

    def project(start, size):
        def tile(i, acc):
            return acc + nt(b2[:, tile_at(i)], xs[start : start + size, tile_at(i)])

        z = lax.fori_loop(0, D // TILE, tile, jnp.zeros((128, size), F32), unroll=4)
        z = stacked3(z[64:] + z[:64])
        return blocks(sum3(nn(z, k2[start : start + size, :])))

    q_sum = q_sum + project(0, 240)
    for copy in second + third:
        copy.wait_recv()
    grad_pass(240, 240, "more")
    q_sum = q_sum + project(240, 240)
    for copy, start in zip(forwards[0], (480, 576)):
        copy.wait_recv()
        q_sum = q_sum + project(start, 64)
    for copy in forwards[1]:
        copy.wait_recv()
    q_sum = q_sum + project(544, 32)

    def sum_of(slots, me, where, meanwhile):
        copies = [send(slots.at[me], slots.at[me], peer) for peer in where]
        meanwhile()
        for copy in copies:
            copy.wait_recv()
        total = slots[0]
        for i in range(1, 8):
            total = total + slots[i]
        return total

    qa[yi * 2 + c] = q_sum
    qb[xi * 2 + zl] = sum_of(
        qa, yi * 2 + c, y_peer[1:] + y_core_peer + [other_core], lambda: grad_pass(480, 160, "more")
    )
    q_all = sum_of(qb, xi * 2 + zl, x_peer[1:] + x_zl_peer + [other_zl], lambda: None)
    for w in range(2):
        q_out[w] = q_all[w * 32 : (w + 1) * 32]

    scaled = q_all * (1.0 / 64.0)
    q_hi = diagonal(scaled.astype(BF16))
    q_low = diagonal((scaled - scaled.astype(BF16).astype(F32)).astype(BF16))
    q_parts = jnp.concatenate([q_hi, q_hi, q_low, jnp.zeros((64, 256), BF16)], axis=0)

    def stores(i):
        return [
            pltpu.make_async_copy(
                ev.at[tile_at(i), pl.ds(w * 128, 128)], ne_ref.at[w, tile_at(i)], out_sem.at[i, w]
            )
            for w in range(2)
        ]

    def last_tile(i, carry):
        at = tile_at(i)
        ev[at, :] = (g[at, :] - nn(bt[at, :], q_parts)).astype(BF16)
        for copy in stores(i):
            copy.start()
        return carry

    lax.fori_loop(0, D // TILE, last_tile, 0, unroll=2)

    def wait_tile(i, carry):
        for copy in stores(i):
            copy.wait()
        return carry

    lax.fori_loop(0, D // TILE, wait_tile, 0)
    for copy in started:
        if copy is not step6:
            copy.wait_send()


N_PIECES = 8


def hand_on(p_ref, q_ref, ne_ref, p_out, q_out, ne_out, held, in_sem, out_sem):
    size = D // N_PIECES
    pieces = [(w, pl.ds(i * size, size)) for i in range(N_PIECES) for w in range(2)]
    loads = [pltpu.make_async_copy(ne_ref.at[at], held.at[at], in_sem.at[i]) for i, at in enumerate(pieces)]
    stores = [pltpu.make_async_copy(held.at[at], ne_out.at[at], out_sem.at[i]) for i, at in enumerate(pieces)]
    for copy in loads:
        copy.start()
    p_out[...] = p_ref[...]
    q_out[...] = q_ref[...]
    for there, back in zip(loads, stores):
        there.wait()
        back.start()
    for copy in stores:
        copy.wait()


N_COPIES = 64


def local(inputs, kv_grads, error, q_init):
    vmem = pl.BlockSpec(memory_space=pltpu.VMEM)
    anywhere = pl.BlockSpec(memory_space=pl.ANY)
    shapes = (
        jax.ShapeDtypeStruct((2, 32, 128), F32),
        jax.ShapeDtypeStruct((2, 32, 128), F32),
        jax.ShapeDtypeStruct((2, D, 128), BF16),
    )
    results = pl.pallas_call(
        kernel,
        out_shape=shapes,
        in_specs=[anywhere] * 4,
        out_specs=(vmem, vmem, anywhere),
        scratch_shapes=[
            pltpu.VMEM((4 * TOK, D), BF16),
            pltpu.VMEM((4 * TOK, 256), BF16),
            pltpu.VMEM((2, 32, 128), F32),
            pltpu.VMEM((4, 80, 128), F32),
            pltpu.VMEM((4, 80, 128), F32),
            pltpu.VMEM((768, TOK), BF16),
            pltpu.VMEM((256, HALF), F32),
            pltpu.VMEM((256, HALF), F32),
            pltpu.VMEM((256, HALF), F32),
            pltpu.VMEM((3, 256, TILE), F32),
            pltpu.VMEM((3, 256, TILE), F32),
            pltpu.VMEM((256, TILE), F32),
            pltpu.VMEM((256, TILE), F32),
            pltpu.VMEM((3, 256, 128), F32),
            pltpu.VMEM((3, 256, 128), F32),
            pltpu.VMEM((2, 256, 128), F32),
            pltpu.VMEM((7, 64, 128), F32),
            pltpu.VMEM((2, 64, 128), F32),
            pltpu.VMEM((64, TILE), F32),
            pltpu.VMEM((64, TILE), F32),
            pltpu.VMEM((64, D), F32),
            pltpu.VMEM((128, D), BF16),
            pltpu.VMEM((D, 256), BF16),
            pltpu.VMEM((D, 256), BF16),
            pltpu.VMEM((D, 256), F32),
            pltpu.VMEM((8, 64, 128), F32),
            pltpu.VMEM((8, 64, 128), F32),
            pltpu.SemaphoreType.DMA((N_COPIES,)),
            pltpu.SemaphoreType.DMA((N_COPIES,)),
            pltpu.SemaphoreType.DMA((12,)),
            pltpu.SemaphoreType.DMA((D // TILE, 2)),
        ],
        compiler_params=pltpu.CompilerParams(
            collective_id=0, has_side_effects=True, vmem_limit_bytes=60 * 1024 * 1024
        ),
    )(inputs, kv_grads, error[:, 0], jnp.swapaxes(q_init, 1, 2))
    p_t, q_t, new_error = pl.pallas_call(
        hand_on,
        out_shape=shapes,
        in_specs=[vmem, vmem, anywhere],
        out_specs=(vmem, vmem, anywhere),
        scratch_shapes=[
            pltpu.VMEM((2, D, 128), BF16),
            pltpu.SemaphoreType.DMA((2 * N_PIECES,)),
            pltpu.SemaphoreType.DMA((2 * N_PIECES,)),
        ],
        compiler_params=pltpu.CompilerParams(vmem_limit_bytes=60 * 1024 * 1024),
    )(*results)
    return (jnp.swapaxes(p_t, 1, 2), jnp.swapaxes(q_t, 1, 2), new_error[:, None])


def solution(mesh):
    in_specs = (
        P(("dp", "tensor"), None),
        P(None, "dp", "tensor"),
        P(None, "dp", None, "tensor"),
        P(None, "tensor", None),
    )
    out_specs = (P(None, "dp", "tensor"), P(None, "tensor", None), P(None, "dp", None, "tensor"))
    return jax.shard_map(local, mesh=mesh, in_specs=in_specs, out_specs=out_specs, check_vma=False)
```

```python
import functools

import jax
import jax.numpy as jnp
from jax import lax
from jax.experimental import pallas as pl
from jax.experimental.pallas import tpu as pltpu
from jax.sharding import PartitionSpec as P

MESH = pl.DeviceIdType.MESH
F32 = jnp.float32
BF16 = jnp.bfloat16

D = 8192
HALF = D // 2
TOK = 160
TILE = 512


def nt(a, b):
    return lax.dot_general(a, b, (((1,), (1,)), ((), ())), preferred_element_type=F32)


def tn(a, b):
    return lax.dot_general(a, b, (((0,), (0,)), ((), ())), preferred_element_type=F32)


def nn(a, b):
    return jnp.dot(a, b, preferred_element_type=F32)


def parts3(a):
    hi = a.astype(BF16)
    rest = a - hi.astype(F32)
    mid = rest.astype(BF16)
    low = (rest - mid.astype(F32)).astype(BF16)
    return hi, mid, low


def stacked3(a):
    return jnp.concatenate(parts3(a), axis=0)


def sum3(r):
    n = r.shape[0] // 3
    return (r[2 * n :] + r[n : 2 * n]) + r[:n]


def whitener(gram):
    rows = lax.broadcasted_iota(jnp.int32, (2, 32, 64), 1)
    cols = lax.broadcasted_iota(jnp.int32, (2, 32, 64), 2)
    eye = jnp.where(
        lax.broadcasted_iota(jnp.int32, (32, 32), 0) == lax.broadcasted_iota(jnp.int32, (32, 32), 1), 1.0, 0.0
    ).astype(F32)
    a = jnp.stack(
        [
            jnp.concatenate([gram[:32, :32], eye], axis=1),
            jnp.concatenate([gram[32:, 32:], eye], axis=1),
        ]
    )
    for j in range(31):
        scale = a[:, :, j : j + 1] / a[:, j : j + 1, j : j + 1]
        a = a - jnp.where(rows > j, scale * a[:, j : j + 1, :], 0.0)
    pivots = jnp.sum(jnp.where(rows == cols, a, 0.0), axis=2, keepdims=True)
    w = a[:, :, 32:] * (1.0 / jnp.sqrt(pivots))
    zero = jnp.zeros((32, 32), F32)
    return jnp.concatenate(
        [jnp.concatenate([w[0], zero], axis=1), jnp.concatenate([zero, w[1]], axis=1)], axis=0
    )


def diagonal(m):
    none = jnp.zeros((32, m.shape[1]), m.dtype)
    return jnp.concatenate(
        [jnp.concatenate([m[:32], none], axis=1), jnp.concatenate([none, m[32:]], axis=1)], axis=0
    )


def blocks(m):
    n = m.shape[1] // 2
    return jnp.concatenate([m[:32, :n], m[32:, n:]], axis=0)


def kernel(
    x_ref, k_ref, e_ref, q_ref, p_out, q_out, merged_out, bt_out,
    xs, k2, qv, ks, kr, kl, fo, fp, rc, ra, rb, a1, b1, ra2, rb2, ab, rz, fab, ga, gb, ft, b2, bt, ev, g,
    qa, qb, send_sem, recv_sem, local_sem, out_sem,
):
    t = lax.axis_index("tensor")
    dp = lax.axis_index("dp")
    c = lax.rem(dp, 2)
    yi = lax.rem(lax.div(dp, 2), 4)
    xi = lax.rem(lax.div(dp, 8), 4)
    zl = lax.div(dp, 32)
    zi = 2 * t + zl

    def device(x=xi, y=yi, z=zi, core=c):
        return {"dp": lax.rem(z, 2) * 32 + x * 8 + y * 2 + core, "tensor": lax.div(z, 2)}

    other_core = device(core=1 - c)
    other_zl = device(z=2 * t + 1 - zl)
    x_peer = [None] + [device(x=lax.rem(xi + o, 4)) for o in (1, 2, 3)]
    y_peer = [None] + [device(y=lax.rem(yi + o, 4)) for o in (1, 2, 3)]
    z_peer = [None] + [device(z=lax.rem(zi + o, 8)) for o in range(1, 8)]
    y_core_peer = [device(y=lax.rem(yi + o, 4), core=1 - c) for o in (1, 2, 3)]
    x_zl_peer = [device(x=lax.rem(xi + o, 4), z=2 * t + 1 - zl) for o in (1, 2, 3)]
    t_right, t_left = z_peer[2], z_peer[6]

    barrier = pltpu.get_barrier_semaphore()
    peers = [other_core] + x_peer[1:] + y_peer[1:] + z_peer[1:] + y_core_peer + x_zl_peer
    for peer in peers:
        pl.semaphore_signal(barrier, inc=1, device_id=peer, device_id_type=MESH)

    started = []

    def send(src, dst, where):
        i = len(started)
        copy = pltpu.make_async_remote_copy(
            src_ref=src, dst_ref=dst, send_sem=send_sem.at[i], recv_sem=recv_sem.at[i],
            device_id=where, device_id_type=MESH,
        )
        copy.start()
        started.append(copy)
        return copy

    def load(src, dst, i):
        copy = pltpu.make_async_copy(src, dst, local_sem.at[i])
        copy.start()
        return copy

    def tile_at(i):
        return pl.ds(pl.multiple_of(i * TILE, TILE), TILE)

    owners = [t, lax.rem(t + 3, 4), lax.rem(t + 1, 4), lax.rem(t + 2, 4)]
    loads = [load(q_ref, qv, 0)]
    for slot in range(4):
        there = pl.ds(pl.multiple_of(owners[slot] * TOK, 16), TOK)
        for w in range(2):
            here = k2.at[pl.ds(slot * TOK, TOK), pl.ds(w * 128, 128)]
            loads.append(load(k_ref.at[w, there], here, 1 + 2 * slot + w))
    load_x = load(x_ref, xs.at[pl.ds(0, TOK)], 9)
    load_e = [load(e_ref.at[w], ev.at[:, pl.ds(w * 128, 128)], 10 + w) for w in range(2)]

    pl.semaphore_wait(barrier, len(peers))

    def rows(start, size):
        return xs.at[pl.ds(start, size)]

    def token_pair(to_right, to_left, size):
        return (
            send(x_ref.at[pl.ds(to_right, size)], rows(TOK + to_right, size), t_right),
            send(x_ref.at[pl.ds(to_left, size)], rows(2 * TOK + to_left, size), t_left),
        )

    first = token_pair(0, 80, 16)

    for copy in loads:
        copy.wait()
    none = jnp.zeros((32, 128), F32)
    q3 = stacked3(
        jnp.concatenate(
            [jnp.concatenate([qv[0], none], axis=1), jnp.concatenate([none, qv[1]], axis=1)], axis=0
        )
    )
    kq = []
    for slot, o in ((3, 4), (1, 6), (2, 2), (0, 0)):
        r = sum3(nt(q3, k2[slot * TOK : (slot + 1) * TOK, :]))
        ref = ks.at[slot] if o else kr.at[t]
        ref[0:64, :] = r[:, 0:128]
        for i in range(4):
            ref[64:80, 32 * i : 32 * i + 32] = r[16 * i : 16 * i + 16, 128:TOK]
        if o:
            kq.append(send(ks.at[slot], kr.at[t], z_peer[o]))

    first = first + token_pair(16, 96, 64)

    load_x.wait()
    for copy in load_e:
        copy.wait()
    for copy in kq:
        copy.wait_recv()
    for s in range(4):
        for i, part in enumerate(parts3(kr[s, 0:64, :])):
            kl[i * 256 + s * 64 : i * 256 + s * 64 + 64, 0:128] = part
        for i, part in enumerate(parts3(kr[s, 64:80, :])):
            for j in range(4):
                at = i * 256 + s * 64 + j * 16
                kl[at : at + 16, 128:TOK] = part[:, 32 * j : 32 * j + 32]
    mine = pl.ds(pl.multiple_of(t * 64, 64), 64)

    def factor_tile(ref, at, there):
        at = pl.ds(at, TILE)
        ref[:, at] = sum3(nn(kl[...], xs[0:TOK, pl.ds(there, TILE)]))
        ref[mine, at] += sum3(nt(q3, ev[pl.ds(there, TILE), :]))

    core_copies = []
    for piece in range(2):

        def partner_tile(i, carry, piece=piece):
            at = pl.multiple_of(piece * 2048 + i * TILE, TILE)
            factor_tile(fp, at, pl.multiple_of((1 - c) * HALF + at, TILE))
            return carry

        lax.fori_loop(0, 4, partner_tile, 0, unroll=2)
        part = pl.ds(piece * 2048, 2048)
        core_copies.append(send(fp.at[:, part], rc.at[:, part], other_core))

    def own_tile(i, carry):
        at = pl.multiple_of(i * TILE, TILE)
        factor_tile(fo, at, pl.multiple_of(c * HALF + at, TILE))
        return carry

    lax.fori_loop(0, 8, own_tile, 0, unroll=2)

    for copy in core_copies:
        copy.wait_recv()

    def add_core(start):
        def some_rows(i, carry):
            r = pl.ds(pl.multiple_of(i * 32, 32), 32)
            fo[r, pl.ds(start, TILE)] += rc[r, pl.ds(start, TILE)]
            return carry

        lax.fori_loop(0, 8, some_rows, 0)

    step1 = []
    for o in (2, 1, 3, 0):
        at_x = pl.multiple_of(lax.rem(xi + o, 4) * TILE, TILE)
        at_y = pl.multiple_of(2048 + lax.rem(yi + o, 4) * TILE, TILE)
        add_core(at_x)
        if o:
            step1.append(send(fo.at[:, pl.ds(at_x, TILE)], ra.at[o - 1], x_peer[o]))
        add_core(at_y)
        if o:
            step1.append(send(fo.at[:, pl.ds(at_y, TILE)], rb.at[o - 1], y_peer[o]))
    for copy in step1:
        copy.wait_recv()

    at_x = pl.multiple_of(xi * TILE, TILE)
    at_y = pl.multiple_of(2048 + yi * TILE, TILE)

    def sum_step1(i, carry):
        r = pl.ds(pl.multiple_of(i * 32, 32), 32)
        a1[r, :] = ((fo[r, pl.ds(at_x, TILE)] + ra[0, r, :]) + ra[1, r, :]) + ra[2, r, :]
        b1[r, :] = ((fo[r, pl.ds(at_y, TILE)] + rb[0, r, :]) + rb[1, r, :]) + rb[2, r, :]
        return carry

    lax.fori_loop(0, 8, sum_step1, 0)

    step2 = []
    for o in (2, 1, 3):
        to_y = pl.ds(pl.multiple_of(lax.rem(yi + o, 4) * 128, 128), 128)
        to_x = pl.ds(pl.multiple_of(lax.rem(xi + o, 4) * 128, 128), 128)
        step2.append(send(a1.at[:, to_y], ra2.at[o - 1], y_peer[o]))
        step2.append(send(b1.at[:, to_x], rb2.at[o - 1], x_peer[o]))
    for copy in step2:
        copy.wait_recv()
    at_y = pl.ds(pl.multiple_of(yi * 128, 128), 128)
    at_x = pl.ds(pl.multiple_of(xi * 128, 128), 128)
    ab[0] = ((a1[:, at_y] + ra2[0]) + ra2[1]) + ra2[2]
    ab[1] = ((b1[:, at_x] + rb2[0]) + rb2[1]) + rb2[2]

    step3 = []
    for o in (4, 3, 5, 2, 6, 1, 7):
        z = lax.rem(zi + o, 8)
        there = pl.ds(pl.multiple_of(lax.div(z, 2) * 64, 64), 64)
        step3.append(send(ab.at[lax.rem(z, 2), there], rz.at[o - 1], z_peer[o]))
    second = token_pair(80, 48, 32)
    for copy in step3:
        copy.wait_recv()
    total = ab[zl, mine, :]
    for o in range(7):
        total = total + rz[o]
    fab[zl] = total
    zl_copy = send(fab.at[zl], fab.at[zl], other_zl)
    third = token_pair(112, 0, 48)

    for copy in first:
        copy.wait_recv()
    forwards = [
        (send(rows(160, 64), rows(480, 64), t_right), send(rows(416, 64), rows(576, 64), t_left)),
        (send(rows(224, 16), rows(544, 16), t_right), send(rows(400, 16), rows(560, 16), t_left)),
    ]

    def grad_pass(start, size, mode):
        k = k2[start : start + size, :]

        def tile(i, carry):
            at = tile_at(i)
            more = tn(xs[start : start + size, at], k)
            if mode == "first":
                g[at, :] = more + ev[at, :].astype(F32)
            else:
                g[at, :] += more
            if mode == "last":
                store(i).start()
            return carry

        lax.fori_loop(0, D // TILE, tile, 0, unroll=4)

    def store(i):
        return pltpu.make_async_copy(g.at[tile_at(i)], merged_out.at[tile_at(i)], out_sem.at[i])

    grad_pass(0, 240, "first")

    zl_copy.wait_recv()
    step4 = []
    for o in (2, 1, 3):
        step4.append(send(fab.at[0], ga.at[:, at_y], y_peer[o]))
        step4.append(send(fab.at[1], gb.at[:, at_x], x_peer[o]))
    ga[:, at_y] = fab[0]
    gb[:, at_x] = fab[1]
    for copy in step4:
        copy.wait_recv()
    own_a = pl.ds(pl.multiple_of(c * HALF + xi * TILE, TILE), TILE)
    own_b = pl.ds(pl.multiple_of(c * HALF + 2048 + yi * TILE, TILE), TILE)
    step5 = []
    for o in (2, 1, 3):
        step5.append(send(ga, ft.at[:, own_a], x_peer[o]))
        step5.append(send(gb, ft.at[:, own_b], y_peer[o]))
    ft[:, own_a] = ga[...]
    ft[:, own_b] = gb[...]
    for copy in step5:
        copy.wait_recv()
    own_half = pl.ds(pl.multiple_of(c * HALF, HALF), HALF)
    step6 = send(ft.at[:, own_half], ft.at[:, own_half], other_core)
    step6.wait()

    def gram_of(acc):
        rows3 = acc[0:64] + acc[64:128] + acc[128:192]
        return rows3[:, 0:64] + rows3[:, 64:128] + rows3[:, 128:192]

    def thrice(w):
        return jnp.concatenate([jnp.concatenate([p, p, p], axis=1) for p in parts3(w)], axis=0)

    def gram_tile(i, acc):
        f = stacked3(ft[:, tile_at(i)])
        return acc + nt(f, f)

    none = jnp.zeros((192, 192), F32)
    w1 = thrice(whitener(gram_of(lax.fori_loop(0, D // TILE, gram_tile, none, unroll=4))))

    def first_round(i, acc):
        b = sum3(nn(w1, stacked3(ft[:, tile_at(i)])))
        ft[:, tile_at(i)] = b
        b = stacked3(b)
        return acc + nt(b, b)

    w2 = thrice(whitener(gram_of(lax.fori_loop(0, D // TILE, first_round, none, unroll=4))))

    def second_round(i, carry):
        b = sum3(nn(w2, stacked3(ft[:, tile_at(i)])))
        ft[:, tile_at(i)] = b
        hi = b.astype(BF16)
        rest = b - hi.astype(F32)
        b2[0:64, tile_at(i)] = hi
        b2[64:128, tile_at(i)] = rest.astype(BF16)
        bt[tile_at(i), :] = jnp.concatenate([b, rest], axis=0).T.astype(BF16)
        return carry

    lax.fori_loop(0, D // TILE, second_round, 0, unroll=4)
    store_bt = load(bt, bt_out, 12)
    own_rows = pl.ds(pl.multiple_of(dp * 128, 128), 128)
    store_p = [load(ft.at[pl.ds(w * 32, 32), own_rows], p_out.at[w], 13 + w) for w in range(2)]

    def error_tile(i, acc):
        return acc + nn(b2[:, tile_at(i)], ev[tile_at(i), :])

    by_w = lax.fori_loop(0, D // TILE, error_tile, jnp.zeros((128, 256), F32), unroll=4)
    q_sum = blocks(by_w[64:] + by_w[:64])

    def project(start, size, unroll=4):
        def tile(i, acc):
            return acc + nt(b2[:, tile_at(i)], xs[start : start + size, tile_at(i)])

        z = lax.fori_loop(0, D // TILE, tile, jnp.zeros((128, size), F32), unroll=unroll)
        z = stacked3(z[64:] + z[:64])
        return blocks(sum3(nn(z, k2[start : start + size, :])))

    q_sum = q_sum + project(0, 240)
    for copy in second + third:
        copy.wait_recv()
    grad_pass(240, 240, "more")
    q_sum = q_sum + project(240, 240)
    last = forwards[0] + forwards[1]
    for copy in started:
        if copy is not step6 and not any(copy is other for other in last):
            copy.wait_send()
    for copy, start in zip(forwards[0], (480, 576)):
        copy.wait_recv()
        q_sum = q_sum + project(start, 64)
    for copy in forwards[1]:
        copy.wait_recv()
    q_sum = q_sum + project(544, 32, 16)

    early = len(started)

    def far_first(six):
        return [six[i] for i in (4, 1, 3, 5, 0, 2)]

    def sum_of(slots, me, where, meanwhile):
        copies = [send(slots.at[me], slots.at[me], peer) for peer in where]
        meanwhile()
        for copy in copies:
            copy.wait_recv()
        total = slots[0]
        for i in range(1, 8):
            total = total + slots[i]
        return total

    qa[yi * 2 + c] = q_sum
    qb[xi * 2 + zl] = sum_of(
        qa, yi * 2 + c, far_first(y_peer[1:] + y_core_peer) + [other_core], lambda: grad_pass(480, 160, "last")
    )
    q_all = sum_of(qb, xi * 2 + zl, far_first(x_peer[1:] + x_zl_peer) + [other_zl], lambda: None)
    for w in range(2):
        qv[w] = q_all[w * 32 : (w + 1) * 32]
    store_q = load(qv, q_out, 15)

    def wait_tile(i, carry):
        store(i).wait()
        return carry

    lax.fori_loop(0, D // TILE, wait_tile, 0)
    for copy in [store_bt, store_q] + store_p:
        copy.wait()
    for copy in list(last) + started[early:]:
        copy.wait_send()


TILE2 = 1024


def update(p_ref, q_ref, merged_ref, bt_ref, p_out, q_out, ne_out, q, m, b, ne, m_sem, b_sem, out_sem, small_sem):
    def at(i):
        return pl.ds(pl.multiple_of(i * TILE2, TILE2), TILE2)

    def loads(i):
        return [
            pltpu.make_async_copy(bt_ref.at[at(i)], b.at[at(i)], b_sem.at[i]),
            pltpu.make_async_copy(merged_ref.at[at(i)], m.at[at(i)], m_sem.at[i]),
        ]

    def store(i):
        return pltpu.make_async_copy(ne.at[:, at(i)], ne_out.at[:, at(i)], out_sem.at[i])

    load_q = pltpu.make_async_copy(q_ref, q, small_sem.at[0])
    load_q.start()
    for i in range(D // TILE2):
        for copy in loads(i):
            copy.start()
    hand_on = [
        pltpu.make_async_copy(p_ref, p_out, small_sem.at[1]),
        pltpu.make_async_copy(q_ref, q_out, small_sem.at[2]),
    ]
    for copy in hand_on:
        copy.start()
    load_q.wait()
    scaled = jnp.concatenate([q[0], q[1]], axis=0) * (1.0 / 64.0)
    q_hi = diagonal(scaled.astype(BF16))
    q_low = diagonal((scaled - scaled.astype(BF16).astype(F32)).astype(BF16))
    q_parts = jnp.concatenate([q_hi, q_hi, q_low, jnp.zeros((64, 256), BF16)], axis=0)

    def tile(i, carry):
        for copy in loads(i):
            copy.wait()
        twice = jnp.concatenate([b[at(i), :], b[at(i), :]], axis=1)
        rest = (m[at(i), :] - nn(twice, q_parts)).astype(BF16)
        for w in range(2):
            ne[w, at(i), :] = rest[:, w * 128 : (w + 1) * 128]
        store(i).start()
        return carry

    lax.fori_loop(0, D // TILE2, tile, 0)

    def wait_tile(i, carry):
        store(i).wait()
        return carry

    lax.fori_loop(0, D // TILE2, wait_tile, 0)
    for copy in hand_on:
        copy.wait()


N_COPIES = 64


def local(inputs, kv_grads, error, q_init):
    anywhere = pl.BlockSpec(memory_space=pl.ANY)
    small = jax.ShapeDtypeStruct((2, 32, 128), F32)
    results = pl.pallas_call(
        kernel,
        out_shape=(small, small, jax.ShapeDtypeStruct((D, 256), F32), jax.ShapeDtypeStruct((D, 128), BF16)),
        in_specs=[anywhere] * 4,
        out_specs=(anywhere,) * 4,
        scratch_shapes=[
            pltpu.VMEM((4 * TOK, D), BF16),
            pltpu.VMEM((4 * TOK, 256), BF16),
            pltpu.VMEM((2, 32, 128), F32),
            pltpu.VMEM((4, 80, 128), F32),
            pltpu.VMEM((4, 80, 128), F32),
            pltpu.VMEM((768, TOK), BF16),
            pltpu.VMEM((256, HALF), F32),
            pltpu.VMEM((256, HALF), F32),
            pltpu.VMEM((256, HALF), F32),
            pltpu.VMEM((3, 256, TILE), F32),
            pltpu.VMEM((3, 256, TILE), F32),
            pltpu.VMEM((256, TILE), F32),
            pltpu.VMEM((256, TILE), F32),
            pltpu.VMEM((3, 256, 128), F32),
            pltpu.VMEM((3, 256, 128), F32),
            pltpu.VMEM((2, 256, 128), F32),
            pltpu.VMEM((7, 64, 128), F32),
            pltpu.VMEM((2, 64, 128), F32),
            pltpu.VMEM((64, TILE), F32),
            pltpu.VMEM((64, TILE), F32),
            pltpu.VMEM((64, D), F32),
            pltpu.VMEM((128, D), BF16),
            pltpu.VMEM((D, 128), BF16),
            pltpu.VMEM((D, 256), BF16),
            pltpu.VMEM((D, 256), F32),
            pltpu.VMEM((8, 64, 128), F32),
            pltpu.VMEM((8, 64, 128), F32),
            pltpu.SemaphoreType.DMA((N_COPIES,)),
            pltpu.SemaphoreType.DMA((N_COPIES,)),
            pltpu.SemaphoreType.DMA((16,)),
            pltpu.SemaphoreType.DMA((D // TILE,)),
        ],
        compiler_params=pltpu.CompilerParams(
            collective_id=0, has_side_effects=True, vmem_limit_bytes=60 * 1024 * 1024
        ),
    )(inputs, kv_grads, error[:, 0], jnp.swapaxes(q_init, 1, 2))
    p_t, q_t, new_error = pl.pallas_call(
        update,
        out_shape=(small, small, jax.ShapeDtypeStruct((2, D, 128), BF16)),
        in_specs=[anywhere] * 4,
        out_specs=(anywhere,) * 3,
        scratch_shapes=[
            pltpu.VMEM((2, 32, 128), F32),
            pltpu.VMEM((D, 256), F32),
            pltpu.VMEM((D, 128), BF16),
            pltpu.VMEM((2, D, 128), BF16),
            pltpu.SemaphoreType.DMA((D // TILE,)),
            pltpu.SemaphoreType.DMA((D // TILE,)),
            pltpu.SemaphoreType.DMA((D // TILE,)),
            pltpu.SemaphoreType.DMA((3,)),
        ],
        compiler_params=pltpu.CompilerParams(vmem_limit_bytes=60 * 1024 * 1024),
    )(*results)
    return (jnp.swapaxes(p_t, 1, 2), jnp.swapaxes(q_t, 1, 2), new_error[:, None])


def solution(mesh):
    in_specs = (
        P(("dp", "tensor"), None),
        P(None, "dp", "tensor"),
        P(None, "dp", None, "tensor"),
        P(None, "tensor", None),
    )
    out_specs = (P(None, "dp", "tensor"), P(None, "tensor", None), P(None, "dp", None, "tensor"))
    return jax.shard_map(local, mesh=mesh, in_specs=in_specs, out_specs=out_specs, check_vma=False)
```

```python
import functools

import jax
import jax.numpy as jnp
from jax import lax
from jax.experimental import pallas as pl
from jax.experimental.pallas import tpu as pltpu
from jax.sharding import PartitionSpec as P

MESH = pl.DeviceIdType.MESH
F32 = jnp.float32
BF16 = jnp.bfloat16

D = 8192
HALF = D // 2
TOK = 160
TILE = 512


def nt(a, b):
    return lax.dot_general(a, b, (((1,), (1,)), ((), ())), preferred_element_type=F32)


def tn(a, b):
    return lax.dot_general(a, b, (((0,), (0,)), ((), ())), preferred_element_type=F32)


def nn(a, b):
    return jnp.dot(a, b, preferred_element_type=F32)


def parts3(a):
    hi = a.astype(BF16)
    rest = a - hi.astype(F32)
    mid = rest.astype(BF16)
    low = (rest - mid.astype(F32)).astype(BF16)
    return hi, mid, low


def stacked3(a):
    return jnp.concatenate(parts3(a), axis=0)


def sum3(r):
    n = r.shape[0] // 3
    return (r[2 * n :] + r[n : 2 * n]) + r[:n]


def whitener(gram):
    rows = lax.broadcasted_iota(jnp.int32, (2, 32, 64), 1)
    cols = lax.broadcasted_iota(jnp.int32, (2, 32, 64), 2)
    eye = jnp.where(
        lax.broadcasted_iota(jnp.int32, (32, 32), 0) == lax.broadcasted_iota(jnp.int32, (32, 32), 1), 1.0, 0.0
    ).astype(F32)
    a = jnp.stack(
        [
            jnp.concatenate([gram[:32, :32], eye], axis=1),
            jnp.concatenate([gram[32:, 32:], eye], axis=1),
        ]
    )
    for j in range(31):
        scale = a[:, :, j : j + 1] / a[:, j : j + 1, j : j + 1]
        a = a - jnp.where(rows > j, scale * a[:, j : j + 1, :], 0.0)
    pivots = jnp.sum(jnp.where(rows == cols, a, 0.0), axis=2, keepdims=True)
    w = a[:, :, 32:] * (1.0 / jnp.sqrt(pivots))
    zero = jnp.zeros((32, 32), F32)
    return jnp.concatenate(
        [jnp.concatenate([w[0], zero], axis=1), jnp.concatenate([zero, w[1]], axis=1)], axis=0
    )


def diagonal(m):
    none = jnp.zeros((32, m.shape[1]), m.dtype)
    return jnp.concatenate(
        [jnp.concatenate([m[:32], none], axis=1), jnp.concatenate([none, m[32:]], axis=1)], axis=0
    )


def blocks(m):
    n = m.shape[1] // 2
    return jnp.concatenate([m[:32, :n], m[32:, n:]], axis=0)


def kernel(
    x_ref, k_ref, e_ref, q_ref, p_out, q_out, merged_out, bt_out,
    xs, k2, qv, ks, kr, kl, fo, fp, rc, ra, rb, a1, b1, ra2, rb2, ab, rz, fab, ga, gb, ft, b2, bt, ev, g,
    qa, qb, send_sem, recv_sem, local_sem, out_sem,
):
    t = lax.axis_index("tensor")
    dp = lax.axis_index("dp")
    c = lax.rem(dp, 2)
    yi = lax.rem(lax.div(dp, 2), 4)
    xi = lax.rem(lax.div(dp, 8), 4)
    zl = lax.div(dp, 32)
    zi = 2 * t + zl

    def device(x=xi, y=yi, z=zi, core=c):
        return {"dp": lax.rem(z, 2) * 32 + x * 8 + y * 2 + core, "tensor": lax.div(z, 2)}

    other_core = device(core=1 - c)
    other_zl = device(z=2 * t + 1 - zl)
    x_peer = [None] + [device(x=lax.rem(xi + o, 4)) for o in (1, 2, 3)]
    y_peer = [None] + [device(y=lax.rem(yi + o, 4)) for o in (1, 2, 3)]
    z_peer = [None] + [device(z=lax.rem(zi + o, 8)) for o in range(1, 8)]
    y_core_peer = [device(y=lax.rem(yi + o, 4), core=1 - c) for o in (1, 2, 3)]
    x_zl_peer = [device(x=lax.rem(xi + o, 4), z=2 * t + 1 - zl) for o in (1, 2, 3)]
    t_right, t_left = z_peer[2], z_peer[6]

    barrier = pltpu.get_barrier_semaphore()
    peers = [other_core] + x_peer[1:] + y_peer[1:] + z_peer[1:] + y_core_peer + x_zl_peer
    for peer in peers:
        pl.semaphore_signal(barrier, inc=1, device_id=peer, device_id_type=MESH)

    started = []

    def send(src, dst, where):
        i = len(started)
        copy = pltpu.make_async_remote_copy(
            src_ref=src, dst_ref=dst, send_sem=send_sem.at[i], recv_sem=recv_sem.at[i],
            device_id=where, device_id_type=MESH,
        )
        copy.start()
        started.append(copy)
        return copy

    def load(src, dst, i):
        copy = pltpu.make_async_copy(src, dst, local_sem.at[i])
        copy.start()
        return copy

    def tile_at(i):
        return pl.ds(pl.multiple_of(i * TILE, TILE), TILE)

    owners = [t, lax.rem(t + 3, 4), lax.rem(t + 1, 4), lax.rem(t + 2, 4)]
    loads = [load(q_ref, qv, 0)]
    for slot in range(4):
        there = pl.ds(pl.multiple_of(owners[slot] * TOK, 16), TOK)
        for w in range(2):
            here = k2.at[pl.ds(slot * TOK, TOK), pl.ds(w * 128, 128)]
            loads.append(load(k_ref.at[w, there], here, 1 + 2 * slot + w))
    load_x = load(x_ref, xs.at[pl.ds(0, TOK)], 9)
    load_e = [load(e_ref.at[w], ev.at[:, pl.ds(w * 128, 128)], 10 + w) for w in range(2)]

    pl.semaphore_wait(barrier, len(peers))

    def rows(start, size):
        return xs.at[pl.ds(start, size)]

    def token_pair(to_right, to_left, size):
        return (
            send(x_ref.at[pl.ds(to_right, size)], rows(TOK + to_right, size), t_right),
            send(x_ref.at[pl.ds(to_left, size)], rows(2 * TOK + to_left, size), t_left),
        )

    first = token_pair(0, 80, 16)

    for copy in loads:
        copy.wait()
    none = jnp.zeros((32, 128), F32)
    q3 = stacked3(
        jnp.concatenate(
            [jnp.concatenate([qv[0], none], axis=1), jnp.concatenate([none, qv[1]], axis=1)], axis=0
        )
    )
    kq = []
    for slot, o in ((3, 4), (1, 6), (2, 2), (0, 0)):
        r = sum3(nt(q3, k2[slot * TOK : (slot + 1) * TOK, :]))
        ref = ks.at[slot] if o else kr.at[t]
        ref[0:64, :] = r[:, 0:128]
        for i in range(4):
            ref[64:80, 32 * i : 32 * i + 32] = r[16 * i : 16 * i + 16, 128:TOK]
        if o:
            kq.append(send(ks.at[slot], kr.at[t], z_peer[o]))

    first = first + token_pair(16, 96, 64)

    load_x.wait()
    for copy in load_e:
        copy.wait()
    for copy in kq:
        copy.wait_recv()
    for s in range(4):
        for i, part in enumerate(parts3(kr[s, 0:64, :])):
            kl[i * 256 + s * 64 : i * 256 + s * 64 + 64, 0:128] = part
        for i, part in enumerate(parts3(kr[s, 64:80, :])):
            for j in range(4):
                at = i * 256 + s * 64 + j * 16
                kl[at : at + 16, 128:TOK] = part[:, 32 * j : 32 * j + 32]
    mine = pl.ds(pl.multiple_of(t * 64, 64), 64)

    def factor_tile(ref, at, there):
        at = pl.ds(at, TILE)
        ref[:, at] = sum3(nn(kl[...], xs[0:TOK, pl.ds(there, TILE)]))
        ref[mine, at] += sum3(nt(q3, ev[pl.ds(there, TILE), :]))

    core_copies = []
    for piece in range(2):

        def partner_tile(i, carry, piece=piece):
            at = pl.multiple_of(piece * 2048 + i * TILE, TILE)
            factor_tile(fp, at, pl.multiple_of((1 - c) * HALF + at, TILE))
            return carry

        lax.fori_loop(0, 4, partner_tile, 0, unroll=2)
        part = pl.ds(piece * 2048, 2048)
        core_copies.append(send(fp.at[:, part], rc.at[:, part], other_core))

    def own_tile(i, carry):
        at = pl.multiple_of(i * TILE, TILE)
        factor_tile(fo, at, pl.multiple_of(c * HALF + at, TILE))
        return carry

    lax.fori_loop(0, 8, own_tile, 0, unroll=2)

    for copy in core_copies:
        copy.wait_recv()

    def add_core(start):
        def some_rows(i, carry):
            r = pl.ds(pl.multiple_of(i * 32, 32), 32)
            fo[r, pl.ds(start, TILE)] += rc[r, pl.ds(start, TILE)]
            return carry

        lax.fori_loop(0, 8, some_rows, 0)

    step1 = []
    for o in (2, 1, 3, 0):
        at_x = pl.multiple_of(lax.rem(xi + o, 4) * TILE, TILE)
        at_y = pl.multiple_of(2048 + lax.rem(yi + o, 4) * TILE, TILE)
        add_core(at_x)
        if o:
            step1.append(send(fo.at[:, pl.ds(at_x, TILE)], ra.at[o - 1], x_peer[o]))
        add_core(at_y)
        if o:
            step1.append(send(fo.at[:, pl.ds(at_y, TILE)], rb.at[o - 1], y_peer[o]))
    for copy in step1:
        copy.wait_recv()

    at_x = pl.multiple_of(xi * TILE, TILE)
    at_y = pl.multiple_of(2048 + yi * TILE, TILE)

    def sum_step1(i, carry):
        r = pl.ds(pl.multiple_of(i * 32, 32), 32)
        a1[r, :] = ((fo[r, pl.ds(at_x, TILE)] + ra[0, r, :]) + ra[1, r, :]) + ra[2, r, :]
        b1[r, :] = ((fo[r, pl.ds(at_y, TILE)] + rb[0, r, :]) + rb[1, r, :]) + rb[2, r, :]
        return carry

    lax.fori_loop(0, 8, sum_step1, 0)

    step2 = []
    for o in (2, 1, 3):
        to_y = pl.ds(pl.multiple_of(lax.rem(yi + o, 4) * 128, 128), 128)
        to_x = pl.ds(pl.multiple_of(lax.rem(xi + o, 4) * 128, 128), 128)
        step2.append(send(a1.at[:, to_y], ra2.at[o - 1], y_peer[o]))
        step2.append(send(b1.at[:, to_x], rb2.at[o - 1], x_peer[o]))
    for copy in step2:
        copy.wait_recv()
    at_y = pl.ds(pl.multiple_of(yi * 128, 128), 128)
    at_x = pl.ds(pl.multiple_of(xi * 128, 128), 128)
    ab[0] = ((a1[:, at_y] + ra2[0]) + ra2[1]) + ra2[2]
    ab[1] = ((b1[:, at_x] + rb2[0]) + rb2[1]) + rb2[2]

    step3 = []
    for o in (4, 3, 5, 2, 6, 1, 7):
        z = lax.rem(zi + o, 8)
        there = pl.ds(pl.multiple_of(lax.div(z, 2) * 64, 64), 64)
        step3.append(send(ab.at[lax.rem(z, 2), there], rz.at[o - 1], z_peer[o]))
    second = token_pair(80, 48, 32)
    for copy in step3:
        copy.wait_recv()
    total = ab[zl, mine, :]
    for o in range(7):
        total = total + rz[o]
    fab[zl] = total
    zl_copy = send(fab.at[zl], fab.at[zl], other_zl)
    third = token_pair(112, 0, 48)

    for copy in first:
        copy.wait_recv()
    forwards = [
        (send(rows(160, 64), rows(480, 64), t_right), send(rows(416, 64), rows(576, 64), t_left)),
        (send(rows(224, 16), rows(544, 16), t_right), send(rows(400, 16), rows(560, 16), t_left)),
    ]

    def grad_pass(start, size, mode):
        k = k2[start : start + size, :]

        def tile(i, carry):
            at = tile_at(i)
            more = tn(xs[start : start + size, at], k)
            if mode == "first":
                g[at, :] = more + ev[at, :].astype(F32)
            else:
                g[at, :] += more
            if mode == "last":
                store(i).start()
            return carry

        lax.fori_loop(0, D // TILE, tile, 0, unroll=4)

    def store(i):
        return pltpu.make_async_copy(g.at[tile_at(i)], merged_out.at[tile_at(i)], out_sem.at[i])

    grad_pass(0, 240, "first")

    zl_copy.wait_recv()
    step4 = []
    for o in (2, 1, 3):
        step4.append(send(fab.at[0], ga.at[:, at_y], y_peer[o]))
        step4.append(send(fab.at[1], gb.at[:, at_x], x_peer[o]))
    ga[:, at_y] = fab[0]
    gb[:, at_x] = fab[1]
    for copy in step4:
        copy.wait_recv()
    own_a = pl.ds(pl.multiple_of(c * HALF + xi * TILE, TILE), TILE)
    own_b = pl.ds(pl.multiple_of(c * HALF + 2048 + yi * TILE, TILE), TILE)
    step5 = []
    for o in (2, 1, 3):
        step5.append(send(ga, ft.at[:, own_a], x_peer[o]))
        step5.append(send(gb, ft.at[:, own_b], y_peer[o]))
    ft[:, own_a] = ga[...]
    ft[:, own_b] = gb[...]
    for copy in step5:
        copy.wait_recv()
    own_half = pl.ds(pl.multiple_of(c * HALF, HALF), HALF)
    step6 = send(ft.at[:, own_half], ft.at[:, own_half], other_core)
    step6.wait()

    def gram_of(acc):
        rows3 = acc[0:64] + acc[64:128] + acc[128:192]
        return rows3[:, 0:64] + rows3[:, 64:128] + rows3[:, 128:192]

    def thrice(w):
        return jnp.concatenate([jnp.concatenate([p, p, p], axis=1) for p in parts3(w)], axis=0)

    def gram_tile(i, acc):
        f = stacked3(ft[:, tile_at(i)])
        return acc + nt(f, f)

    none = jnp.zeros((192, 192), F32)
    w1 = thrice(whitener(gram_of(lax.fori_loop(0, D // TILE, gram_tile, none, unroll=4))))

    def first_round(i, acc):
        b = sum3(nn(w1, stacked3(ft[:, tile_at(i)])))
        ft[:, tile_at(i)] = b
        b = stacked3(b)
        return acc + nt(b, b)

    w2 = thrice(whitener(gram_of(lax.fori_loop(0, D // TILE, first_round, none, unroll=4))))

    def second_round(i, carry):
        b = sum3(nn(w2, stacked3(ft[:, tile_at(i)])))
        ft[:, tile_at(i)] = b
        hi = b.astype(BF16)
        rest = b - hi.astype(F32)
        b2[0:64, tile_at(i)] = hi
        b2[64:128, tile_at(i)] = rest.astype(BF16)
        bt[tile_at(i), :] = jnp.concatenate([b, rest], axis=0).T.astype(BF16)
        return carry

    lax.fori_loop(0, D // TILE, second_round, 0, unroll=4)
    store_bt = load(bt, bt_out, 12)
    own_rows = pl.ds(pl.multiple_of(dp * 128, 128), 128)
    store_p = [load(ft.at[pl.ds(w * 32, 32), own_rows], p_out.at[w], 13 + w) for w in range(2)]

    def error_tile(i, acc):
        return acc + nn(b2[:, tile_at(i)], ev[tile_at(i), :])

    by_w = lax.fori_loop(0, D // TILE, error_tile, jnp.zeros((128, 256), F32), unroll=4)
    q_sum = blocks(by_w[64:] + by_w[:64])

    def project(start, size, unroll=4):
        def tile(i, acc):
            return acc + nt(b2[:, tile_at(i)], xs[start : start + size, tile_at(i)])

        z = lax.fori_loop(0, D // TILE, tile, jnp.zeros((128, size), F32), unroll=unroll)
        z = stacked3(z[64:] + z[:64])
        return blocks(sum3(nn(z, k2[start : start + size, :])))

    q_sum = q_sum + project(0, 240)
    for copy in second + third:
        copy.wait_recv()
    grad_pass(240, 240, "more")
    q_sum = q_sum + project(240, 240)
    last = forwards[0] + forwards[1]
    for copy in started:
        if copy is not step6 and not any(copy is other for other in last):
            copy.wait_send()
    for copy, start in zip(forwards[0], (480, 576)):
        copy.wait_recv()
        q_sum = q_sum + project(start, 64)
    for copy in forwards[1]:
        copy.wait_recv()
    q_sum = q_sum + project(544, 32, 16)

    early = len(started)

    def far_first(six):
        return [six[i] for i in (4, 1, 3, 5, 0, 2)]

    def sum_of(slots, me, where, meanwhile):
        copies = [send(slots.at[me], slots.at[me], peer) for peer in where]
        meanwhile()
        for copy in copies:
            copy.wait_recv()
        total = slots[0]
        for i in range(1, 8):
            total = total + slots[i]
        return total

    qa[yi * 2 + c] = q_sum
    qb[xi * 2 + zl] = sum_of(
        qa, yi * 2 + c, far_first(y_peer[1:] + y_core_peer) + [other_core], lambda: grad_pass(480, 160, "last")
    )
    q_all = sum_of(qb, xi * 2 + zl, far_first(x_peer[1:] + x_zl_peer) + [other_zl], lambda: None)
    for w in range(2):
        qv[w] = q_all[w * 32 : (w + 1) * 32]
    store_q = load(qv, q_out, 15)

    def wait_tile(i, carry):
        store(i).wait()
        return carry

    lax.fori_loop(0, D // TILE, wait_tile, 0)
    for copy in [store_bt, store_q] + store_p:
        copy.wait()
    for copy in list(last) + started[early:]:
        copy.wait_send()


TILE2 = 2048


def update(p_ref, q_ref, merged_ref, bt_ref, p_out, q_out, ne_out, q, m, b, ne, m_sem, b_sem, out_sem, small_sem):
    def at(i):
        return pl.ds(pl.multiple_of(i * TILE2, TILE2), TILE2)

    def loads(i):
        return [
            pltpu.make_async_copy(bt_ref.at[at(i)], b.at[at(i)], b_sem.at[i]),
            pltpu.make_async_copy(merged_ref.at[at(i)], m.at[at(i)], m_sem.at[i]),
        ]

    def store(i):
        return pltpu.make_async_copy(ne.at[:, at(i)], ne_out.at[:, at(i)], out_sem.at[i])

    load_q = pltpu.make_async_copy(q_ref, q, small_sem.at[0])
    load_q.start()
    for i in range(D // TILE2):
        for copy in loads(i):
            copy.start()
    hand_on = [
        pltpu.make_async_copy(p_ref, p_out, small_sem.at[1]),
        pltpu.make_async_copy(q_ref, q_out, small_sem.at[2]),
    ]
    for copy in hand_on:
        copy.start()
    load_q.wait()
    scaled = jnp.concatenate([q[0], q[1]], axis=0) * (1.0 / 64.0)
    q_hi = diagonal(scaled.astype(BF16))
    q_low = diagonal((scaled - scaled.astype(BF16).astype(F32)).astype(BF16))
    q_parts = jnp.concatenate([q_hi, q_hi, q_low, jnp.zeros((64, 256), BF16)], axis=0)

    def tile(i, carry):
        for copy in loads(i):
            copy.wait()
        twice = jnp.concatenate([b[at(i), :], b[at(i), :]], axis=1)
        rest = (m[at(i), :] - nn(twice, q_parts)).astype(BF16)
        for w in range(2):
            ne[w, at(i), :] = rest[:, w * 128 : (w + 1) * 128]
        store(i).start()
        return carry

    lax.fori_loop(0, D // TILE2, tile, 0)

    def wait_tile(i, carry):
        store(i).wait()
        return carry

    lax.fori_loop(0, D // TILE2, wait_tile, 0)
    for copy in hand_on:
        copy.wait()


N_COPIES = 64


def local(inputs, kv_grads, error, q_init):
    anywhere = pl.BlockSpec(memory_space=pl.ANY)
    small = jax.ShapeDtypeStruct((2, 32, 128), F32)
    results = pl.pallas_call(
        kernel,
        out_shape=(small, small, jax.ShapeDtypeStruct((D, 256), F32), jax.ShapeDtypeStruct((D, 128), BF16)),
        in_specs=[anywhere] * 4,
        out_specs=(anywhere,) * 4,
        scratch_shapes=[
            pltpu.VMEM((4 * TOK, D), BF16),
            pltpu.VMEM((4 * TOK, 256), BF16),
            pltpu.VMEM((2, 32, 128), F32),
            pltpu.VMEM((4, 80, 128), F32),
            pltpu.VMEM((4, 80, 128), F32),
            pltpu.VMEM((768, TOK), BF16),
            pltpu.VMEM((256, HALF), F32),
            pltpu.VMEM((256, HALF), F32),
            pltpu.VMEM((256, HALF), F32),
            pltpu.VMEM((3, 256, TILE), F32),
            pltpu.VMEM((3, 256, TILE), F32),
            pltpu.VMEM((256, TILE), F32),
            pltpu.VMEM((256, TILE), F32),
            pltpu.VMEM((3, 256, 128), F32),
            pltpu.VMEM((3, 256, 128), F32),
            pltpu.VMEM((2, 256, 128), F32),
            pltpu.VMEM((7, 64, 128), F32),
            pltpu.VMEM((2, 64, 128), F32),
            pltpu.VMEM((64, TILE), F32),
            pltpu.VMEM((64, TILE), F32),
            pltpu.VMEM((64, D), F32),
            pltpu.VMEM((128, D), BF16),
            pltpu.VMEM((D, 128), BF16),
            pltpu.VMEM((D, 256), BF16),
            pltpu.VMEM((D, 256), F32),
            pltpu.VMEM((8, 64, 128), F32),
            pltpu.VMEM((8, 64, 128), F32),
            pltpu.SemaphoreType.DMA((N_COPIES,)),
            pltpu.SemaphoreType.DMA((N_COPIES,)),
            pltpu.SemaphoreType.DMA((16,)),
            pltpu.SemaphoreType.DMA((D // TILE,)),
        ],
        compiler_params=pltpu.CompilerParams(
            collective_id=0, has_side_effects=True, vmem_limit_bytes=60 * 1024 * 1024
        ),
    )(inputs, kv_grads, error[:, 0], jnp.swapaxes(q_init, 1, 2))
    p_t, q_t, new_error = pl.pallas_call(
        update,
        out_shape=(small, small, jax.ShapeDtypeStruct((2, D, 128), BF16)),
        in_specs=[anywhere] * 4,
        out_specs=(anywhere,) * 3,
        scratch_shapes=[
            pltpu.VMEM((2, 32, 128), F32),
            pltpu.VMEM((D, 256), F32),
            pltpu.VMEM((D, 128), BF16),
            pltpu.VMEM((2, D, 128), BF16),
            pltpu.SemaphoreType.DMA((D // TILE,)),
            pltpu.SemaphoreType.DMA((D // TILE,)),
            pltpu.SemaphoreType.DMA((D // TILE,)),
            pltpu.SemaphoreType.DMA((3,)),
        ],
        compiler_params=pltpu.CompilerParams(vmem_limit_bytes=60 * 1024 * 1024),
    )(*results)
    return (jnp.swapaxes(p_t, 1, 2), jnp.swapaxes(q_t, 1, 2), new_error[:, None])


def solution(mesh):
    in_specs = (
        P(("dp", "tensor"), None),
        P(None, "dp", "tensor"),
        P(None, "dp", None, "tensor"),
        P(None, "tensor", None),
    )
    out_specs = (P(None, "dp", "tensor"), P(None, "tensor", None), P(None, "dp", None, "tensor"))
    return jax.shard_map(local, mesh=mesh, in_specs=in_specs, out_specs=out_specs, check_vma=False)
```
